512 devices in a mesh: slab: 256 (over y, x, z), col: 2 (over core).
Axes of the slice: x: 4, y: 4, z: 16, core: 2. Of those that a mesh axis runs over, the one named last changes fastest.
Arguments:
- displacement: float32 [3, 1024, 128, 256], P(None, 'slab', 'col'), may hold values from -6 to 6
- velocity: float32 [3, 1024, 128, 256], P(None, 'slab', 'col'), may hold values from -6 to 6
- damage: float32 [1024, 128, 256], P('slab', 'col'), may hold values from 0.5 to 1.5
- broken: int32 [2, 1024, 128, 256], P(None, 'slab', 'col'), may hold values from 0 to 255, as said below
- counts: int32 [256, 4], replicated, may hold values from 0 to 64, as said below
- bits: int32 [4], replicated, may hold values from 0 to 3, each once
Outputs:
- relocated: float32 [6, 1024, 128, 256], P(None, 'slab', 'col')
The draws below stay inside these ranges and needn't reach their ends.
Inputs may be any that keep to these rules, and one draw needn't show every extreme that they name: Each bit of a plane of broken marks one forward bond as broken. `counts`: in every aligned group of 16 slabs, the slabs at offsets 0, 1, 2, 4 and 8 of the group offer 64 columns in every round. `bits`: each bit 0..3 is used in exactly one round.
All inputs are finite; a program needn't handle non-finite values.
Results may differ from the reference program's by a relative error of at most 0.00002.
Values sent between devices are 32-bit elements; how exact they have to be, the bound alone decides.
No kernel may reach another device: no remote copies, remote signals or barrier semaphores. Data moves between devices by JAX's collectives and lax.ppermute only.
A program may use at most 64 MiB of HBM per device.

```python
import math
import jax
import jax.numpy as jnp

CX = 4
CYH = 64
ROUNDS = 4
SLABS = 256
MAXC = 64
NX = 1024
NY = 128
NZ = 256
N_COL = 2


def draw_broken(key, part):
    total = jnp.zeros((2, NX, NY, NZ), jnp.int32)
    for index in range(8):
        picked = jax.random.randint(jax.random.fold_in(key, index), (2, NX, NY, NZ), 0, 20)
        total = total + jnp.left_shift(jnp.where(picked < 3, 1, 0).astype(jnp.int32), index)
    chosen = jax.random.randint(jax.random.fold_in(key, 99), (), 0, NX * NY * NZ)
    flat_index = jnp.arange(NX * NY * NZ, dtype=jnp.int32).reshape(1, NX, NY, NZ)
    return jnp.where(flat_index == chosen, 255, total).astype(jnp.int32)


def draw_counts(key, part):
    base = jax.random.randint(key, (SLABS, ROUNDS), 0, MAXC + 1)
    place = jnp.arange(SLABS) % 16
    filled = (place == 0) | (place == 1) | (place == 2) | (place == 4) | (place == 8)
    return jnp.where(filled[:, None], MAXC, base).astype(jnp.int32)


def shard_levels(own_key, extent, split, least, high):
    factor_of, own = 1.0, jax.random.fold_in(own_key, 6)
    for position, shards_of in split:
        heights = jnp.exp(jax.random.uniform(jax.random.fold_in(own, position), (shards_of,), jnp.float32, least / len(split), high / len(split)))
        factor_of = factor_of * jnp.repeat(heights, extent[position] // shards_of).reshape([-1 if axis == position else 1 for axis in range(len(extent))])
    return factor_of


def centred(own_key, shape, scale, most, split=(), kind=jnp.bfloat16):
    values = scale * jax.random.normal(own_key, shape, jnp.float32)
    if split:
        values = values * shard_levels(own_key, shape, split, -0.22, 0.18)
    return jnp.clip(values, -most, most).astype(kind)


def setup_inputs(seed: int = 0) -> dict:
    streams_of = jax.random.split(jax.random.key(seed), 7)
    displacement = centred(streams_of[0], (3, NX, NY, NZ), 1.0, 6.0, ((1, 256), (2, 2)), jnp.float32)
    velocity = centred(streams_of[1], (3, NX, NY, NZ), 1.0, 6.0, ((1, 256), (2, 2)), jnp.float32)
    damage = jnp.clip(0.5 + 1.0 * jax.random.uniform(streams_of[2], (NX, NY, NZ), jnp.float32) ** shard_levels(streams_of[2], (NX, NY, NZ), ((0, 256), (1, 2)), -0.2, 0.2), 0.5, 1.5)
    broken = draw_broken(jax.random.fold_in(streams_of[6], 71), 0)
    counts = draw_counts(jax.random.fold_in(streams_of[6], 71), 0)
    bits = jax.random.permutation(streams_of[5], ROUNDS).astype(jnp.int32)
    return {"displacement": displacement, "velocity": velocity, "damage": damage, "broken": broken, "counts": counts, "bits": bits}


def bond_table():
    table = []
    for step_x in range(-2, 3):
        for step_y in range(-2, 3):
            for step_z in range(-2, 3):
                square = step_x * step_x + step_y * step_y + step_z * step_z
                if 0 < square <= 4 and (step_x, step_y, step_z) > (0, 0, 0):
                    length = math.sqrt(square)
                    table.append((step_x, step_y, step_z, (1.0 - length / 2.5) / length ** 3))
    return table

def reference(displacement, velocity, damage, broken, counts, bits):
    extent_x, extent_y, extent_z = damage.shape
    moved = jnp.pad(displacement, ((0, 0), (2, 2), (2, 2), (2, 2)))
    scaled = jnp.pad(damage, 2)
    flags = jnp.pad(broken, ((0, 0), (2, 2), (2, 2), (2, 2)))
    force = jnp.zeros(displacement.shape, jnp.float32)
    for index, (step_x, step_y, step_z, weight) in enumerate(bond_table()):
        plane_index = index // 8
        bit_index = index % 8
        for sign in (1, -1):
            low_x, low_y, low_z = (2 + sign * step_x, 2 + sign * step_y, 2 + sign * step_z)
            other = moved[:, low_x:low_x + extent_x, low_y:low_y + extent_y, low_z:low_z + extent_z]
            other_scale = scaled[low_x:low_x + extent_x, low_y:low_y + extent_y, low_z:low_z + extent_z]
            if sign == 1:
                source = broken[plane_index]
            else:
                source = flags[plane_index, low_x:low_x + extent_x, low_y:low_y + extent_y, low_z:low_z + extent_z]
            alive = 1.0 - jnp.bitwise_and(jnp.right_shift(source, bit_index), 1).astype(jnp.float32)
            along = step_x * (other[0] - displacement[0]) + step_y * (other[1] - displacement[1]) + step_z * (other[2] - displacement[2])
            factor = weight * damage * other_scale * alive * along
            force = force + jnp.stack([factor * step_x, factor * step_y, factor * step_z])
    new_velocity = velocity + 0.1 * force
    new_displacement = displacement + 0.1 * new_velocity
    state = jnp.concatenate([new_displacement, new_velocity], 0)
    blocks = state.reshape(6, SLABS, CX, N_COL, CYH, extent_z).transpose(1, 3, 0, 2, 4, 5)
    blocks = blocks.reshape(SLABS, N_COL, 6, CX * CYH, extent_z)
    device = jnp.arange(SLABS, dtype=jnp.int32)
    column = jnp.arange(CX * CYH, dtype=jnp.int32)
    for round_index in range(ROUNDS):
        shift = jnp.left_shift(jnp.int32(1), bits[round_index].astype(jnp.int32)).astype(jnp.int32)
        partner = jnp.bitwise_xor(device, shift).astype(jnp.int32)
        taken = jnp.minimum(counts[:, round_index], jnp.take(counts[:, round_index], partner))
        other = jnp.take(blocks, partner, axis=0)
        keep = column[None, :] < taken[:, None]
        blocks = jnp.where(keep[:, None, None, :, None], other, blocks)
    blocks = blocks.reshape(SLABS, N_COL, 6, CX, CYH, extent_z).transpose(2, 0, 3, 1, 4, 5)
    return blocks.reshape(6, extent_x, extent_y, extent_z)
```

```python
import functools
import math

import jax
import jax.numpy as jnp
from jax import lax
from jax.experimental import pallas as pl
from jax.experimental.pallas import tpu as pltpu
from jax.sharding import PartitionSpec as P

GROUP = 16
LANES = 128
TOP = 8


def bond_table():
    table = []
    for step_x in range(-2, 3):
        for step_y in range(-2, 3):
            for step_z in range(-2, 3):
                square = step_x * step_x + step_y * step_y + step_z * step_z
                if 0 < square <= 4 and (step_x, step_y, step_z) > (0, 0, 0):
                    length = math.sqrt(square)
                    table.append((step_x, step_y, step_z, (1.0 - length / 2.5) / length**3))
    return table


BONDS = bond_table()


def to_groups(ref, component, rows, halves):
    group = rows // 4
    for half, value in enumerate(halves):
        low = component * 8 + half * 4
        ref[group, low : low + 4, :] = value[0:4]
        ref[group + 1, low : low + 4, :] = value[4:8]


def alive_of(flags, index):
    return (flags & (1 << (index % 8))) == 0


def pack_kernel(disp, damage, broken, up, down, edge, edge_up, edge_down, send):
    position = lax.axis_index("col")
    planes, rows = damage.shape[0], damage.shape[1]
    last = planes - 1
    for c in range(3):
        up[c] = disp[c, last]
        down[c] = disp[c, 0]
    up[3] = damage[last]
    up[4] = broken[0, last].astype(jnp.float32)
    up[5] = broken[1, last].astype(jnp.float32)
    up[6] = disp[0, last - 1]
    up[7] = jnp.where(alive_of(broken[1, last - 1], 15), damage[last - 1], 0.0)
    down[3] = damage[0]
    down[4] = disp[0, 1]
    down[5] = damage[1]
    edge_up[...] = jnp.zeros(edge_up.shape, jnp.float32)
    edge_down[...] = jnp.zeros(edge_down.shape, jnp.float32)

    def edges(first, inner):
        for plane in range(planes):
            at = slice(2 * plane, 2 * plane + 2)
            for c in range(3):
                edge[c, at] = disp[c, plane, first : first + 2]
            edge[3, at] = damage[plane, first : first + 2]
            for word in range(2):
                edge[4 + word, at] = broken[word, plane, first : first + 2].astype(jnp.float32)
        one = slice(inner, inner + 1)
        for c in range(3):
            edge_up[c : c + 1] = disp[c, last, one]
            edge_down[c : c + 1] = disp[c, 0, one]
        edge_up[3:4] = damage[last, one]
        edge_down[3:4] = damage[0, one]
        for word in range(2):
            edge_up[4 + word : 5 + word] = broken[word, last, one].astype(jnp.float32)

    @pl.when(position == 0)
    def _():
        edges(rows - 2, rows - 1)

    @pl.when(position == 1)
    def _():
        edges(0, 0)

    for c in range(3):
        for start in range(0, rows, 8):
            to_groups(
                send,
                c,
                start,
                [disp[c, 0, start : start + 8, h * LANES : (h + 1) * LANES] for h in range(2)],
            )


def fill(fields, flags, slot, values, words, rim, width, position, rows):
    lane = lax.broadcasted_iota(jnp.int32, (rows + 2 * TOP, LANES), 1)

    def base(ref, index, read, rim_read, dtype):
        ref[index, 2, slot, :, 0:TOP] = jnp.zeros((2, TOP, LANES), dtype)
        ref[index, 2, slot, :, TOP + rows :] = jnp.zeros((2, TOP, LANES), dtype)
        for half in range(2):
            cells = slice(half * LANES, (half + 1) * LANES)
            ref[index, 2, slot, half, TOP : TOP + rows] = read(cells)

        @pl.when(position == 0)
        def _():
            for half in range(2):
                cells = slice(half * LANES, (half + 1) * LANES)
                ref[index, 2, slot, half, TOP + rows : TOP + rows + width] = rim_read(cells)

        @pl.when(position == 1)
        def _():
            for half in range(2):
                cells = slice(half * LANES, (half + 1) * LANES)
                ref[index, 2, slot, half, TOP - width : TOP] = rim_read(cells)

    def shift(ref, index, amounts, zero):
        halves = [ref[index, 2, slot, half] for half in range(2)]
        for amount in amounts:
            rolled = [pltpu.roll(v, (-amount) % LANES, 1) for v in halves]
            crossed = lane >= LANES - amount if amount > 0 else lane < -amount
            edge = jnp.zeros_like(rolled[0]) if zero else rolled[0]
            if amount > 0:
                new = [jnp.where(crossed, rolled[1], rolled[0]), jnp.where(crossed, edge, rolled[1])]
            else:
                new = [jnp.where(crossed, edge, rolled[0]), jnp.where(crossed, rolled[0], rolled[1])]
            for half in range(2):
                ref[index, 2 + amount, slot, half] = new[half]

    for index, (read, rim_read) in enumerate(zip(values, rim[:4])):
        base(fields, index, read, rim_read, jnp.float32)
        shift(fields, index, (-2, -1, 1, 2) if index >= 2 else (-1, 1), index == 3)
    for index, (read, rim_read) in enumerate(zip(words, rim[4:])):
        base(flags, index, read, rim_read, jnp.int32)
        shift(flags, index, (-2, -1, 1) if index == 0 else (-1, 1), False)


def force_kernel(
    targets, disp, vel, damage, broken, up, down, edge, edge_up, edge_down, out, fields, flags
):
    position = lax.axis_index("col")
    planes, rows = damage.shape[0], damage.shape[1]
    needed = sorted({p + a for p in targets for a in (-1, 0, 1)})
    slots = {p: slot for slot, p in enumerate(needed)}

    for p in needed:
        if p < 0:
            values = [lambda cells, c=c: up[c, :, cells] for c in range(4)]
            words = [lambda cells, w=w: up[4 + w, :, cells].astype(jnp.int32) for w in range(2)]
            rim = [lambda cells, c=c: edge_up[c : c + 1, cells] for c in range(4)]
            rim += [
                lambda cells, w=w: edge_up[4 + w : 5 + w, cells].astype(jnp.int32) for w in range(2)
            ]
            width = 1
        elif p >= planes:
            values = [lambda cells, c=c: down[c, :, cells] for c in range(4)]
            words = []
            rim = [lambda cells, c=c: edge_down[c : c + 1, cells] for c in range(4)]
            width = 1
        else:
            at = slice(2 * p, 2 * p + 2)
            values = [lambda cells, c=c, p=p: disp[c, p, :, cells] for c in range(3)]
            values += [lambda cells, p=p: damage[p, :, cells]]
            words = [lambda cells, w=w, p=p: broken[w, p, :, cells] for w in range(2)]
            rim = [lambda cells, c=c, at=at: edge[c, at, cells] for c in range(4)]
            rim += [
                lambda cells, w=w, at=at: edge[4 + w, at, cells].astype(jnp.int32) for w in range(2)
            ]
            width = 2
        fill(fields, flags, slots[p], values, words, rim, width, position, rows)

    def block(step, carry):
        start = pl.multiple_of(step * 8, 8)
        own_rows = pl.ds(start, 8)
        for p in targets:
            updated = []
            for half in range(2):
                cells = slice(half * LANES, (half + 1) * LANES)
                own = [disp[c, p, own_rows, cells] for c in range(3)]
                own_damage = damage[p, own_rows, cells]
                own_words = [broken[w, p, own_rows, cells] for w in range(2)]
                force = [None, None, None]

                def add(axis, value):
                    force[axis] = value if force[axis] is None else force[axis] + value

                for index, (step_x, step_y, step_z, weight) in enumerate(BONDS):
                    for sign in (1, -1):
                        if step_x == 2:
                            q = p + 2 * sign
                            if q == -2:
                                other, scale = up[6, own_rows, cells], up[7, own_rows, cells]
                            elif q == -1:
                                other, scale = up[0, own_rows, cells], up[3, own_rows, cells]
                                bits = up[5, own_rows, cells].astype(jnp.int32)
                                scale = jnp.where(alive_of(bits, index), scale, 0.0)
                            elif q == planes + 1:
                                other, scale = down[4, own_rows, cells], down[5, own_rows, cells]
                            elif q == planes:
                                other, scale = down[0, own_rows, cells], down[3, own_rows, cells]
                            else:
                                other, scale = disp[0, q, own_rows, cells], damage[q, own_rows, cells]
                                if sign == -1:
                                    bits = broken[1, q, own_rows, cells]
                                    scale = jnp.where(alive_of(bits, index), scale, 0.0)
                            if sign == 1:
                                scale = jnp.where(alive_of(own_words[1], index), scale, 0.0)
                            factor = (4.0 * weight) * scale * (other - own[0])
                            add(0, factor)
                            continue
                        slot = slots[p + sign * step_x]
                        at = pl.ds(start + TOP + sign * step_y, 8)
                        place = 2 + sign * step_z
                        steps = (step_x, step_y, step_z)
                        along = None
                        for axis in range(3):
                            if steps[axis] == 0:
                                continue
                            part = fields[axis, place, slot, half, at] - own[axis]
                            if abs(steps[axis]) == 2:
                                along = part
                            elif along is None:
                                along = part if steps[axis] == 1 else -part
                            else:
                                along = along + part if steps[axis] == 1 else along - part
                        scale = fields[3, place, slot, half, at]
                        if sign == 1:
                            bits = own_words[index // 8]
                        else:
                            bits = flags[index // 8, place, slot, half, at]
                        scale = jnp.where(alive_of(bits, index), scale, 0.0)
                        if max(abs(s) for s in steps) == 2:
                            factor = (4.0 * weight) * scale * along
                        else:
                            factor = weight * scale * along
                        for axis in range(3):
                            if steps[axis] > 0:
                                add(axis, factor)
                            elif steps[axis] < 0:
                                add(axis, -factor)
                new_velocity = [
                    vel[c, p, own_rows, cells] + 0.1 * (own_damage * force[c]) for c in range(3)
                ]
                if targets == (0,):
                    updated.append(new_velocity)
                else:
                    for c in range(3):
                        out[3 + c, p, own_rows, cells] = new_velocity[c]
                        out[c, p, own_rows, cells] = own[c] + 0.1 * new_velocity[c]
            if targets == (0,):
                for c in range(3):
                    for half in range(2):
                        low = c * 8 + half * 4
                        out[2 * step, low : low + 4, :] = updated[half][c][0:4]
                        out[2 * step + 1, low : low + 4, :] = updated[half][c][4:8]
        return carry

    lax.fori_loop(0, rows // 8, block, 0)


def route_kernel(taken, bits, data, out, scratch):
    member = lax.rem(lax.axis_index("slab"), GROUP)
    column = 4 * member + lax.rem(lax.broadcasted_iota(jnp.int32, (24, LANES), 0), 4)
    for turn in range(4):
        source = data if turn == 0 else scratch.at[(turn - 1) % 2]
        target = out if turn == 3 else scratch.at[turn % 2]
        distance = jnp.left_shift(jnp.int32(1), bits[turn])
        for slab in range(GROUP):
            moved = column < taken[turn * GROUP + slab]
            target[slab] = jnp.where(moved, source[jnp.bitwise_xor(slab, distance)], source[slab])


def place_kernel(whole, first, second, out):
    del whole
    rows = out.shape[2]
    for start in range(0, rows, 8):
        group = start // 4
        at = slice(start, start + 8)
        for c in range(3):
            for half in range(2):
                cells = slice(half * LANES, (half + 1) * LANES)
                low = c * 8 + half * 4
                part = slice(low, low + 4)
                for g in range(2):
                    at = slice(start + 4 * g, start + 4 * g + 4)
                    velocity = second[group + g, part]
                    out[3 + c, 0, at, cells] = velocity
                    out[c, 0, at, cells] = first[group + g, part] + 0.1 * velocity


VMEM = pl.BlockSpec(memory_space=pltpu.VMEM)
SMEM = pl.BlockSpec(memory_space=pltpu.SMEM)
PARAMS = pltpu.CompilerParams(vmem_limit_bytes=40 * 1024 * 1024)


def exchange(block):
    count = lax.axis_size("slab")
    groups = [list(range(g, g + GROUP)) for g in range(0, count, GROUP)]
    return lax.all_to_all(block, "slab", 0, 0, axis_index_groups=groups)


def on_device(displacement, velocity, damage, broken, counts, bits):
    planes, rows, cells = damage.shape
    f32 = jnp.float32
    shape = jax.ShapeDtypeStruct
    group_shape = (GROUP, 24, LANES)
    up, down, edge, edge_up, edge_down, first = pl.pallas_call(
        pack_kernel,
        out_shape=[
            shape((8, rows, cells), f32),
            shape((6, rows, cells), f32),
            shape((6, 2 * planes, cells), f32),
            shape((8, cells), f32),
            shape((8, cells), f32),
            shape(group_shape, f32),
        ],
        in_specs=[VMEM] * 3,
        out_specs=[VMEM] * 6,
        compiler_params=PARAMS,
        name="pack",
    )(displacement, damage, broken)

    slabs = lax.axis_size("slab")
    upward = [(i, i + 1) for i in range(slabs - 1)]
    downward = [(i + 1, i) for i in range(slabs - 1)]
    across_up = [(2 * s + c, 2 * t + 1 - c) for s, t in upward for c in range(2)]
    across_down = [(2 * s + c, 2 * t + 1 - c) for s, t in downward for c in range(2)]
    both = ("slab", "col")
    up = lax.ppermute(up, "slab", upward)
    edge_up = lax.ppermute(edge_up, both, across_up)
    edge = lax.ppermute(edge, "col", [(0, 1), (1, 0)])
    down = lax.ppermute(down, "slab", downward)
    edge_down = lax.ppermute(edge_down, both, across_down)

    member = jnp.arange(GROUP, dtype=jnp.int32)
    base = lax.axis_index("slab") // GROUP * GROUP
    mine = lax.dynamic_slice_in_dim(counts, base, GROUP, 0).T
    partner = jnp.bitwise_xor(member[None, :], jnp.left_shift(jnp.int32(1), bits)[:, None])
    taken = jnp.minimum(mine, jnp.take_along_axis(mine, partner, axis=1)).reshape(-1)

    def forces(targets, out):
        kept = len(targets) + 2
        return pl.pallas_call(
            functools.partial(force_kernel, targets),
            out_shape=out,
            in_specs=[VMEM] * 9,
            out_specs=VMEM,
            scratch_shapes=[
                pltpu.VMEM((4, 5, kept, 2, rows + 2 * TOP, LANES), f32),
                pltpu.VMEM((2, 5, kept, 2, rows + 2 * TOP, LANES), jnp.int32),
            ],
            compiler_params=PARAMS,
            name="force_first" if targets == (0,) else "force_rest",
        )(displacement, velocity, damage, broken, up, down, edge, edge_up, edge_down)

    def route(data):
        return pl.pallas_call(
            route_kernel,
            out_shape=shape(group_shape, f32),
            in_specs=[SMEM, SMEM, VMEM],
            out_specs=VMEM,
            scratch_shapes=[pltpu.VMEM((2,) + group_shape, f32)],
            compiler_params=PARAMS,
            name="route",
        )(taken, bits, data)

    second = forces((0,), shape(group_shape, f32))
    whole = forces(tuple(range(1, planes)), shape((6, planes, rows, cells), f32))
    first = exchange(route(exchange(first)))
    second = exchange(route(exchange(second)))
    return pl.pallas_call(
        place_kernel,
        out_shape=shape((6, planes, rows, cells), f32),
        in_specs=[pl.BlockSpec(memory_space=pl.ANY)] + [pl.BlockSpec(group_shape, lambda i: (0, 0, 0))] * 2,
        out_specs=pl.BlockSpec((6, 1, rows, cells), lambda i: (0, 0, 0, 0)),
        grid=(1,),
        input_output_aliases={0: 0},
        compiler_params=PARAMS,
        name="place",
    )(whole, first, second)


def solution(mesh):
    return jax.shard_map(
        on_device,
        mesh=mesh,
        in_specs=(
            P(None, "slab", "col", None),
            P(None, "slab", "col", None),
            P("slab", "col", None),
            P(None, "slab", "col", None),
            P(),
            P(),
        ),
        out_specs=P(None, "slab", "col", None),
        check_vma=False,
    )
```

```python
import functools
import math

import jax
import jax.numpy as jnp
from jax import lax
from jax.experimental import pallas as pl
from jax.experimental.pallas import tpu as pltpu
from jax.sharding import PartitionSpec as P

GROUP = 16
LANES = 128
TOP = 8


def bond_table():
    table = []
    for step_x in range(-2, 3):
        for step_y in range(-2, 3):
            for step_z in range(-2, 3):
                square = step_x * step_x + step_y * step_y + step_z * step_z
                if 0 < square <= 4 and (step_x, step_y, step_z) > (0, 0, 0):
                    length = math.sqrt(square)
                    table.append((step_x, step_y, step_z, (1.0 - length / 2.5) / length**3))
    return table


BONDS = bond_table()


def to_groups(ref, step, first, half, values):
    for c, value in enumerate(values):
        low = (first + c) * 8 + half * 4
        ref[2 * step, low : low + 4, :] = value[0:4]
        ref[2 * step + 1, low : low + 4, :] = value[4:8]


def alive_of(flags, index):
    return (flags & (1 << (index % 8))) == 0


def pack_up_kernel(disp, damage, broken, up, words, scale, sems):
    last = damage.shape[0] - 1
    moves = [(disp.at[c, last], up.at[c]) for c in range(3)]
    moves += [(damage.at[last], up.at[3]), (disp.at[0, last - 1], up.at[6])]
    moves += [(broken.at[w, last], words.at[w]) for w in range(2)]
    moves += [(broken.at[1, last - 1], words.at[2]), (damage.at[last - 1], scale)]
    copies = [
        pltpu.make_async_copy(source, target, sems.at[i])
        for i, (source, target) in enumerate(moves)
    ]
    for copy in copies:
        copy.start()
    for copy in copies:
        copy.wait()
    up[4] = words[0].astype(jnp.float32)
    up[5] = words[1].astype(jnp.float32)
    up[7] = jnp.where(alive_of(words[2], 15), scale[...], 0.0)


def pack_rest_kernel(
    disp, damage, broken, order, down, edge, edge_up, edge_down, disp_rim, damage_rim, words, sems
):
    del order
    position = lax.axis_index("col")
    planes, rows = damage.shape[0], damage.shape[1]
    last = planes - 1
    rim = pl.ds(pl.multiple_of((1 - position) * (rows - 8), 8), 8)
    moves = [
        (disp.at[:, :, rim], disp_rim),
        (damage.at[:, rim], damage_rim),
        (broken.at[:, :, rim], words),
        (disp.at[0, 1], down.at[4]),
        (damage.at[0], down.at[3]),
        (damage.at[1], down.at[5]),
    ]
    moves += [(disp.at[c, 0], down.at[c]) for c in range(3)]
    copies = [
        pltpu.make_async_copy(source, target, sems.at[i])
        for i, (source, target) in enumerate(moves)
    ]
    for copy in copies:
        copy.start()
    edge_up[...] = jnp.zeros(edge_up.shape, jnp.float32)
    edge_down[...] = jnp.zeros(edge_down.shape, jnp.float32)
    for copy in copies:
        copy.wait()

    def edges(first, inner):
        for plane in range(planes):
            at = slice(2 * plane, 2 * plane + 2)
            for c in range(3):
                edge[c, at] = disp_rim[c, plane, first : first + 2]
            edge[3, at] = damage_rim[plane, first : first + 2]
            for word in range(2):
                edge[4 + word, at] = words[word, plane, first : first + 2].astype(jnp.float32)
        one = slice(inner, inner + 1)
        for c in range(3):
            edge_up[c : c + 1] = disp_rim[c, last, one]
            edge_down[c : c + 1] = disp_rim[c, 0, one]
        edge_up[3:4] = damage_rim[last, one]
        edge_down[3:4] = damage_rim[0, one]
        for word in range(2):
            edge_up[4 + word : 5 + word] = words[word, last, one].astype(jnp.float32)

    @pl.when(position == 0)
    def _():
        edges(6, 7)

    @pl.when(position == 1)
    def _():
        edges(0, 0)


def fill(fields, flags, slot, values, words, rim, width, position, rows):
    lane = lax.broadcasted_iota(jnp.int32, (rows + 2 * TOP, LANES), 1)

    def base(ref, index, read, rim_read, dtype):
        ref[index, 2, slot, :, 0:TOP] = jnp.zeros((2, TOP, LANES), dtype)
        ref[index, 2, slot, :, TOP + rows :] = jnp.zeros((2, TOP, LANES), dtype)
        for half in range(2):
            cells = slice(half * LANES, (half + 1) * LANES)
            ref[index, 2, slot, half, TOP : TOP + rows] = read(cells)

        @pl.when(position == 0)
        def _():
            for half in range(2):
                cells = slice(half * LANES, (half + 1) * LANES)
                ref[index, 2, slot, half, TOP + rows : TOP + rows + width] = rim_read(cells)

        @pl.when(position == 1)
        def _():
            for half in range(2):
                cells = slice(half * LANES, (half + 1) * LANES)
                ref[index, 2, slot, half, TOP - width : TOP] = rim_read(cells)

    def shift(ref, index, amounts, zero):
        halves = [ref[index, 2, slot, half] for half in range(2)]
        for amount in amounts:
            rolled = [pltpu.roll(v, (-amount) % LANES, 1) for v in halves]
            crossed = lane >= LANES - amount if amount > 0 else lane < -amount
            edge = jnp.zeros_like(rolled[0]) if zero else rolled[0]
            if amount > 0:
                new = [jnp.where(crossed, rolled[1], rolled[0]), jnp.where(crossed, edge, rolled[1])]
            else:
                new = [jnp.where(crossed, edge, rolled[0]), jnp.where(crossed, rolled[0], rolled[1])]
            for half in range(2):
                ref[index, 2 + amount, slot, half] = new[half]

    for index, (read, rim_read) in enumerate(zip(values, rim[:4])):
        base(fields, index, read, rim_read, jnp.float32)
        shift(fields, index, (-2, -1, 1, 2) if index >= 2 else (-1, 1), index == 3)
    for index, (read, rim_read) in enumerate(zip(words, rim[4:])):
        base(flags, index, read, rim_read, jnp.int32)
        shift(flags, index, (-2, -1, 1) if index == 0 else (-1, 1), False)


def force_kernel(targets, low, high, names, *refs):
    ref_of = dict(zip(names, refs))
    out, fields, flags = refs[len(names) :]
    disp, vel, damage = ref_of["disp"], ref_of["vel"], ref_of["damage"]
    broken, up, down = ref_of.get("broken"), ref_of.get("up"), ref_of.get("down")
    edge, edge_up, edge_down = ref_of.get("edge"), ref_of.get("edge_up"), ref_of.get("edge_down")
    position = lax.axis_index("col")
    planes, rows = ref_of["damage"].shape[0], damage.shape[1]
    closing = high == 0
    needed = sorted({p + a for p in targets for a in (-1, 0, 1) if low <= p + a < high})
    slots = {p: slot for slot, p in enumerate(needed)}

    for p in needed:
        if p < 0:
            values = [lambda cells, c=c: up[c, :, cells] for c in range(4)]
            words = [lambda cells, w=w: up[4 + w, :, cells].astype(jnp.int32) for w in range(2)]
            rim = [lambda cells, c=c: edge_up[c : c + 1, cells] for c in range(4)]
            rim += [
                lambda cells, w=w: edge_up[4 + w : 5 + w, cells].astype(jnp.int32) for w in range(2)
            ]
            width = 1
        elif p >= planes:
            values = [lambda cells, c=c: down[c, :, cells] for c in range(4)]
            words = []
            rim = [lambda cells, c=c: edge_down[c : c + 1, cells] for c in range(4)]
            width = 1
        else:
            at = slice(2 * p, 2 * p + 2)
            values = [lambda cells, c=c, p=p: disp[c, p, :, cells] for c in range(3)]
            values += [lambda cells, p=p: damage[p, :, cells]]
            words = [lambda cells, w=w, p=p: broken[w, p, :, cells] for w in range(2)]
            rim = [lambda cells, c=c, at=at: edge[c, at, cells] for c in range(4)]
            rim += [
                lambda cells, w=w, at=at: edge[4 + w, at, cells].astype(jnp.int32) for w in range(2)
            ]
            width = 2
        fill(fields, flags, slots[p], values, words, rim, width, position, rows)

    def block(step, carry):
        start = pl.multiple_of(step * 8, 8)
        own_rows = pl.ds(start, 8)
        for p in targets:
            for half in range(2):
                cells = slice(half * LANES, (half + 1) * LANES)
                own = [disp[c, p, own_rows, cells] for c in range(3)]
                own_damage = damage[p, own_rows, cells]
                own_words = [broken[w, p, own_rows, cells] for w in range(2)] if not closing else []
                force = [None, None, None]

                def add(axis, value):
                    force[axis] = value if force[axis] is None else force[axis] + value

                for index, (step_x, step_y, step_z, weight) in enumerate(BONDS):
                    for sign in (1, -1):
                        if not low <= p + sign * step_x < high:
                            continue
                        if step_x == 2:
                            q = p + 2 * sign
                            if q == -2:
                                other, scale = up[6, own_rows, cells], up[7, own_rows, cells]
                            elif q == -1:
                                other, scale = up[0, own_rows, cells], up[3, own_rows, cells]
                                bits = up[5, own_rows, cells].astype(jnp.int32)
                                scale = jnp.where(alive_of(bits, index), scale, 0.0)
                            elif q == planes + 1:
                                other, scale = down[4, own_rows, cells], down[5, own_rows, cells]
                            elif q == planes:
                                other, scale = down[0, own_rows, cells], down[3, own_rows, cells]
                            else:
                                other, scale = disp[0, q, own_rows, cells], damage[q, own_rows, cells]
                                if sign == -1:
                                    bits = broken[1, q, own_rows, cells]
                                    scale = jnp.where(alive_of(bits, index), scale, 0.0)
                            if sign == 1:
                                scale = jnp.where(alive_of(own_words[1], index), scale, 0.0)
                            factor = (4.0 * weight) * scale * (other - own[0])
                            add(0, factor)
                            continue
                        slot = slots[p + sign * step_x]
                        at = pl.ds(start + TOP + sign * step_y, 8)
                        place = 2 + sign * step_z
                        steps = (step_x, step_y, step_z)
                        along = None
                        for axis in range(3):
                            if steps[axis] == 0:
                                continue
                            part = fields[axis, place, slot, half, at] - own[axis]
                            if abs(steps[axis]) == 2:
                                along = part
                            elif along is None:
                                along = part if steps[axis] == 1 else -part
                            else:
                                along = along + part if steps[axis] == 1 else along - part
                        scale = fields[3, place, slot, half, at]
                        if sign == 1:
                            bits = own_words[index // 8]
                        else:
                            bits = flags[index // 8, place, slot, half, at]
                        scale = jnp.where(alive_of(bits, index), scale, 0.0)
                        if max(abs(s) for s in steps) == 2:
                            factor = (4.0 * weight) * scale * along
                        else:
                            factor = weight * scale * along
                        for axis in range(3):
                            if steps[axis] > 0:
                                add(axis, factor)
                            elif steps[axis] < 0:
                                add(axis, -factor)
                new_velocity = [
                    vel[c, p, own_rows, cells] + 0.1 * (own_damage * force[c]) for c in range(3)
                ]
                if closing:
                    to_groups(out, step, 0, half, new_velocity)
                    to_groups(out, step, 3, half, own)
                elif targets == (0,):
                    for c in range(3):
                        out[c, 0, own_rows, cells] = new_velocity[c]
                else:
                    for c in range(3):
                        out[3 + c, p, own_rows, cells] = new_velocity[c]
                        out[c, p, own_rows, cells] = own[c] + 0.1 * new_velocity[c]
        return carry

    lax.fori_loop(0, rows // 8, block, 0)


def route_kernel(taken, bits, data, out, scratch):
    member = lax.rem(lax.axis_index("slab"), GROUP)
    column = 4 * member + lax.rem(lax.broadcasted_iota(jnp.int32, (48, LANES), 0), 4)
    for turn in range(4):
        source = data if turn == 0 else scratch.at[(turn - 1) % 2]
        target = out if turn == 3 else scratch.at[turn % 2]
        distance = jnp.left_shift(jnp.int32(1), bits[turn])
        for slab in range(GROUP):
            moved = column < taken[turn * GROUP + slab]
            target[slab] = jnp.where(moved, source[jnp.bitwise_xor(slab, distance)], source[slab])


def place_kernel(whole, columns, out):
    del whole
    rows = out.shape[2]
    for start in range(0, rows, 8):
        group = start // 4
        at = slice(start, start + 8)
        for c in range(3):
            for half in range(2):
                cells = slice(half * LANES, (half + 1) * LANES)
                low = c * 8 + half * 4
                part = slice(low, low + 4)
                for g in range(2):
                    at = slice(start + 4 * g, start + 4 * g + 4)
                    velocity = columns[group + g, part]
                    out[3 + c, 0, at, cells] = velocity
                    out[c, 0, at, cells] = columns[group + g, low + 24 : low + 28] + 0.1 * velocity


VMEM = pl.BlockSpec(memory_space=pltpu.VMEM)
SMEM = pl.BlockSpec(memory_space=pltpu.SMEM)
ALONE = pltpu.CompilerParams(vmem_limit_bytes=60 * 1024 * 1024)
PARAMS = pltpu.CompilerParams(vmem_limit_bytes=40 * 1024 * 1024)


def exchange(block):
    count = lax.axis_size("slab")
    groups = [list(range(g, g + GROUP)) for g in range(0, count, GROUP)]
    return lax.all_to_all(block, "slab", 0, 0, axis_index_groups=groups)


def on_device(displacement, velocity, damage, broken, counts, bits):
    planes, rows, cells = damage.shape
    f32 = jnp.float32
    shape = jax.ShapeDtypeStruct
    group_shape = (GROUP, 48, LANES)
    slabs = lax.axis_size("slab")
    upward = [(i, i + 1) for i in range(slabs - 1)]
    downward = [(i + 1, i) for i in range(slabs - 1)]
    across_up = [(2 * s + c, 2 * t + 1 - c) for s, t in upward for c in range(2)]
    across_down = [(2 * s + c, 2 * t + 1 - c) for s, t in downward for c in range(2)]
    both = ("slab", "col")
    anywhere = pl.BlockSpec(memory_space=pl.ANY)

    packed = pl.pallas_call(
        pack_up_kernel,
        out_shape=shape((8, rows, cells), f32),
        in_specs=[pl.BlockSpec(memory_space=pltpu.HBM)] * 3,
        out_specs=VMEM,
        scratch_shapes=[
            pltpu.VMEM((3, rows, cells), jnp.int32),
            pltpu.VMEM((rows, cells), f32),
            pltpu.SemaphoreType.DMA((9,)),
        ],
        compiler_params=ALONE,
        name="pack_up",
    )(displacement, damage, broken)
    up = lax.ppermute(packed, "slab", upward)
    down, edge, edge_up, edge_down = pl.pallas_call(
        pack_rest_kernel,
        out_shape=[
            shape((6, rows, cells), f32),
            shape((6, 2 * planes, cells), f32),
            shape((8, cells), f32),
            shape((8, cells), f32),
        ],
        in_specs=[pl.BlockSpec(memory_space=pltpu.HBM)] * 3 + [anywhere],
        out_specs=[VMEM] * 4,
        scratch_shapes=[
            pltpu.VMEM((3, planes, 8, cells), f32),
            pltpu.VMEM((planes, 8, cells), f32),
            pltpu.VMEM((2, planes, 8, cells), jnp.int32),
            pltpu.SemaphoreType.DMA((9,)),
        ],
        compiler_params=ALONE,
        name="pack_rest",
    )(displacement, damage, broken, packed)
    edge_up = lax.ppermute(edge_up, both, across_up)
    edge = lax.ppermute(edge, "col", [(0, 1), (1, 0)])
    down = lax.ppermute(down, "slab", downward)
    edge_down = lax.ppermute(edge_down, both, across_down)

    member = jnp.arange(GROUP, dtype=jnp.int32)
    base = lax.axis_index("slab") // GROUP * GROUP
    mine = lax.dynamic_slice_in_dim(counts, base, GROUP, 0).T
    partner = jnp.bitwise_xor(member[None, :], jnp.left_shift(jnp.int32(1), bits)[:, None])
    taken = jnp.minimum(mine, jnp.take_along_axis(mine, partner, axis=1)).reshape(-1)

    def forces(name, targets, low, high, out, **operands):
        slots = sum(low <= p < high for p in range(min(targets) - 1, max(targets) + 2))
        return pl.pallas_call(
            functools.partial(force_kernel, targets, low, high, tuple(operands)),
            out_shape=out,
            in_specs=[anywhere if key.startswith("order") else VMEM for key in operands],
            out_specs=VMEM,
            scratch_shapes=[
                pltpu.VMEM((4, 5, slots, 2, rows + 2 * TOP, LANES), f32),
                pltpu.VMEM((2, 5, slots, 2, rows + 2 * TOP, LANES), jnp.int32),
            ],
            compiler_params=PARAMS,
            name=name,
        )(*operands.values())

    own = dict(disp=displacement, damage=damage)
    begun = forces(
        "force_own", (0,), 0, planes, shape((3, 1, rows, cells), f32),
        vel=velocity, broken=broken, edge=edge, **own,
    )
    send = forces(
        "force_below", (0,), -2, 0, shape(group_shape, f32),
        vel=begun, up=up, edge_up=edge_up, order=down, order_edge=edge_down, **own,
    )
    columns = exchange(send)

    whole = forces(
        "force_rest", tuple(range(1, planes)), -2, planes + 2, shape((6, planes, rows, cells), f32),
        vel=velocity, broken=broken, up=up, down=down, edge=edge, edge_up=edge_up,
        edge_down=edge_down, **own,
    )
    columns = pl.pallas_call(
        route_kernel,
        out_shape=shape(group_shape, f32),
        in_specs=[SMEM, SMEM, VMEM],
        out_specs=VMEM,
        scratch_shapes=[pltpu.VMEM((2,) + group_shape, f32)],
        compiler_params=PARAMS,
        name="route",
    )(taken, bits, columns)
    columns = exchange(columns)
    return pl.pallas_call(
        place_kernel,
        out_shape=shape((6, planes, rows, cells), f32),
        in_specs=[anywhere, pl.BlockSpec(group_shape, lambda i: (0, 0, 0))],
        out_specs=pl.BlockSpec((6, 1, rows, cells), lambda i: (0, 0, 0, 0)),
        grid=(1,),
        input_output_aliases={0: 0},
        compiler_params=PARAMS,
        name="place",
    )(whole, columns)


def solution(mesh):
    return jax.shard_map(
        on_device,
        mesh=mesh,
        in_specs=(
            P(None, "slab", "col", None),
            P(None, "slab", "col", None),
            P("slab", "col", None),
            P(None, "slab", "col", None),
            P(),
            P(),
        ),
        out_specs=P(None, "slab", "col", None),
        check_vma=False,
    )
```

```python
import functools
import math

import jax
import jax.numpy as jnp
from jax import lax
from jax.experimental import pallas as pl
from jax.experimental.pallas import tpu as pltpu
from jax.sharding import PartitionSpec as P

GROUP = 16
LANES = 128
TOP = 8


def bond_table():
    table = []
    for step_x in range(-2, 3):
        for step_y in range(-2, 3):
            for step_z in range(-2, 3):
                square = step_x * step_x + step_y * step_y + step_z * step_z
                if 0 < square <= 4 and (step_x, step_y, step_z) > (0, 0, 0):
                    length = math.sqrt(square)
                    table.append((step_x, step_y, step_z, (1.0 - length / 2.5) / length**3))
    return table


BONDS = bond_table()


def to_groups(ref, step, first, half, values):
    for c, value in enumerate(values):
        low = (first + c) * 8 + half * 4
        ref[2 * step, low : low + 4, :] = value[0:4]
        ref[2 * step + 1, low : low + 4, :] = value[4:8]


def alive_of(flags, index):
    return (flags & (1 << (index % 8))) == 0


def pack_kernel(
    disp, damage, broken, up, down, edge, edge_up, edge_down, disp_rim, damage_rim, words, flags,
    scale, sems
):
    position = lax.axis_index("col")
    planes, rows = damage.shape[0], damage.shape[1]
    last = planes - 1
    rim = pl.ds(pl.multiple_of((1 - position) * (rows - 8), 8), 8)
    moves = [
        (disp.at[:, :, rim], disp_rim),
        (damage.at[:, rim], damage_rim),
        (broken.at[:, :, rim], words),
        (disp.at[0, 1], down.at[4]),
        (damage.at[0], down.at[3]),
        (damage.at[1], down.at[5]),
    ]
    moves += [(disp.at[c, 0], down.at[c]) for c in range(3)]
    moves += [(disp.at[c, last], up.at[c]) for c in range(3)]
    moves += [(damage.at[last], up.at[3]), (disp.at[0, last - 1], up.at[6])]
    moves += [(broken.at[w, last], flags.at[w]) for w in range(2)]
    moves += [(broken.at[1, last - 1], flags.at[2]), (damage.at[last - 1], scale)]
    copies = [
        pltpu.make_async_copy(source, target, sems.at[i])
        for i, (source, target) in enumerate(moves)
    ]
    for copy in copies:
        copy.start()
    edge_up[...] = jnp.zeros(edge_up.shape, jnp.float32)
    edge_down[...] = jnp.zeros(edge_down.shape, jnp.float32)
    for copy in copies:
        copy.wait()
    up[4] = flags[0].astype(jnp.float32)
    up[5] = flags[1].astype(jnp.float32)
    up[7] = jnp.where(alive_of(flags[2], 15), scale[...], 0.0)

    def edges(first, inner):
        for plane in range(planes):
            at = slice(2 * plane, 2 * plane + 2)
            for c in range(3):
                edge[c, at] = disp_rim[c, plane, first : first + 2]
            edge[3, at] = damage_rim[plane, first : first + 2]
            for word in range(2):
                edge[4 + word, at] = words[word, plane, first : first + 2].astype(jnp.float32)
        one = slice(inner, inner + 1)
        for c in range(3):
            edge_up[c : c + 1] = disp_rim[c, last, one]
            edge_down[c : c + 1] = disp_rim[c, 0, one]
        edge_up[3:4] = damage_rim[last, one]
        edge_down[3:4] = damage_rim[0, one]
        for word in range(2):
            edge_up[4 + word : 5 + word] = words[word, last, one].astype(jnp.float32)

    @pl.when(position == 0)
    def _():
        edges(6, 7)

    @pl.when(position == 1)
    def _():
        edges(0, 0)


def fill(fields, flags, slot, values, words, rim, width, position, rows):
    lane = lax.broadcasted_iota(jnp.int32, (rows + 2 * TOP, LANES), 1)

    def base(ref, index, read, rim_read, dtype):
        ref[index, 2, slot, :, 0:TOP] = jnp.zeros((2, TOP, LANES), dtype)
        ref[index, 2, slot, :, TOP + rows :] = jnp.zeros((2, TOP, LANES), dtype)
        for half in range(2):
            cells = slice(half * LANES, (half + 1) * LANES)
            ref[index, 2, slot, half, TOP : TOP + rows] = read(cells)

        @pl.when(position == 0)
        def _():
            for half in range(2):
                cells = slice(half * LANES, (half + 1) * LANES)
                ref[index, 2, slot, half, TOP + rows : TOP + rows + width] = rim_read(cells)

        @pl.when(position == 1)
        def _():
            for half in range(2):
                cells = slice(half * LANES, (half + 1) * LANES)
                ref[index, 2, slot, half, TOP - width : TOP] = rim_read(cells)

    def shift(ref, index, amounts, zero):
        halves = [ref[index, 2, slot, half] for half in range(2)]
        for amount in amounts:
            rolled = [pltpu.roll(v, (-amount) % LANES, 1) for v in halves]
            crossed = lane >= LANES - amount if amount > 0 else lane < -amount
            edge = jnp.zeros_like(rolled[0]) if zero else rolled[0]
            if amount > 0:
                new = [jnp.where(crossed, rolled[1], rolled[0]), jnp.where(crossed, edge, rolled[1])]
            else:
                new = [jnp.where(crossed, edge, rolled[0]), jnp.where(crossed, rolled[0], rolled[1])]
            for half in range(2):
                ref[index, 2 + amount, slot, half] = new[half]

    for index, (read, rim_read) in enumerate(zip(values, rim[:4])):
        base(fields, index, read, rim_read, jnp.float32)
        shift(fields, index, (-2, -1, 1, 2) if index >= 2 else (-1, 1), index == 3)
    for index, (read, rim_read) in enumerate(zip(words, rim[4:])):
        base(flags, index, read, rim_read, jnp.int32)
        shift(flags, index, (-2, -1, 1) if index == 0 else (-1, 1), False)


def force_kernel(targets, low, high, names, *refs):
    ref_of = dict(zip(names, refs))
    out, fields, flags = refs[len(names) :]
    disp, vel, damage = ref_of["disp"], ref_of["vel"], ref_of["damage"]
    broken, up, down = ref_of.get("broken"), ref_of.get("up"), ref_of.get("down")
    edge, edge_up, edge_down = ref_of.get("edge"), ref_of.get("edge_up"), ref_of.get("edge_down")
    position = lax.axis_index("col")
    planes, rows = ref_of["damage"].shape[0], damage.shape[1]
    closing = high == 0
    needed = sorted({p + a for p in targets for a in (-1, 0, 1) if low <= p + a < high})
    slots = {p: slot for slot, p in enumerate(needed)}

    for p in needed:
        if p < 0:
            values = [lambda cells, c=c: up[c, :, cells] for c in range(4)]
            words = [lambda cells, w=w: up[4 + w, :, cells].astype(jnp.int32) for w in range(2)]
            rim = [lambda cells, c=c: edge_up[c : c + 1, cells] for c in range(4)]
            rim += [
                lambda cells, w=w: edge_up[4 + w : 5 + w, cells].astype(jnp.int32) for w in range(2)
            ]
            width = 1
        elif p >= planes:
            values = [lambda cells, c=c: down[c, :, cells] for c in range(4)]
            words = []
            rim = [lambda cells, c=c: edge_down[c : c + 1, cells] for c in range(4)]
            width = 1
        else:
            at = slice(2 * p, 2 * p + 2)
            values = [lambda cells, c=c, p=p: disp[c, p, :, cells] for c in range(3)]
            values += [lambda cells, p=p: damage[p, :, cells]]
            words = [lambda cells, w=w, p=p: broken[w, p, :, cells] for w in range(2)]
            rim = [lambda cells, c=c, at=at: edge[c, at, cells] for c in range(4)]
            rim += [
                lambda cells, w=w, at=at: edge[4 + w, at, cells].astype(jnp.int32) for w in range(2)
            ]
            width = 2
        fill(fields, flags, slots[p], values, words, rim, width, position, rows)

    def block(step, carry):
        start = pl.multiple_of(step * 8, 8)
        own_rows = pl.ds(start, 8)
        for p in targets:
            for half in range(2):
                cells = slice(half * LANES, (half + 1) * LANES)
                own = [disp[c, p, own_rows, cells] for c in range(3)]
                own_damage = damage[p, own_rows, cells]
                own_words = [broken[w, p, own_rows, cells] for w in range(2)] if not closing else []
                force = [None, None, None]

                def add(axis, value):
                    force[axis] = value if force[axis] is None else force[axis] + value

                for index, (step_x, step_y, step_z, weight) in enumerate(BONDS):
                    for sign in (1, -1):
                        if not low <= p + sign * step_x < high:
                            continue
                        if step_x == 2:
                            q = p + 2 * sign
                            if q == -2:
                                other, scale = up[6, own_rows, cells], up[7, own_rows, cells]
                            elif q == -1:
                                other, scale = up[0, own_rows, cells], up[3, own_rows, cells]
                                bits = up[5, own_rows, cells].astype(jnp.int32)
                                scale = jnp.where(alive_of(bits, index), scale, 0.0)
                            elif q == planes + 1:
                                other, scale = down[4, own_rows, cells], down[5, own_rows, cells]
                            elif q == planes:
                                other, scale = down[0, own_rows, cells], down[3, own_rows, cells]
                            else:
                                other, scale = disp[0, q, own_rows, cells], damage[q, own_rows, cells]
                                if sign == -1:
                                    bits = broken[1, q, own_rows, cells]
                                    scale = jnp.where(alive_of(bits, index), scale, 0.0)
                            if sign == 1:
                                scale = jnp.where(alive_of(own_words[1], index), scale, 0.0)
                            factor = (4.0 * weight) * scale * (other - own[0])
                            add(0, factor)
                            continue
                        slot = slots[p + sign * step_x]
                        at = pl.ds(start + TOP + sign * step_y, 8)
                        place = 2 + sign * step_z
                        steps = (step_x, step_y, step_z)
                        along = None
                        for axis in range(3):
                            if steps[axis] == 0:
                                continue
                            part = fields[axis, place, slot, half, at] - own[axis]
                            if abs(steps[axis]) == 2:
                                along = part
                            elif along is None:
                                along = part if steps[axis] == 1 else -part
                            else:
                                along = along + part if steps[axis] == 1 else along - part
                        scale = fields[3, place, slot, half, at]
                        if sign == 1:
                            bits = own_words[index // 8]
                        else:
                            bits = flags[index // 8, place, slot, half, at]
                        scale = jnp.where(alive_of(bits, index), scale, 0.0)
                        if max(abs(s) for s in steps) == 2:
                            factor = (4.0 * weight) * scale * along
                        else:
                            factor = weight * scale * along
                        for axis in range(3):
                            if steps[axis] > 0:
                                add(axis, factor)
                            elif steps[axis] < 0:
                                add(axis, -factor)
                new_velocity = [
                    vel[c, p, own_rows, cells] + 0.1 * (own_damage * force[c]) for c in range(3)
                ]
                if closing:
                    to_groups(out, step, 0, half, new_velocity)
                    to_groups(out, step, 3, half, own)
                elif targets == (0,):
                    for c in range(3):
                        out[c, 0, own_rows, cells] = new_velocity[c]
                else:
                    for c in range(3):
                        out[3 + c, p, own_rows, cells] = new_velocity[c]
                        out[c, p, own_rows, cells] = own[c] + 0.1 * new_velocity[c]
        return carry

    lax.fori_loop(0, rows // 8, block, 0)


def route_kernel(taken, bits, data, order, out, scratch):
    del order
    member = lax.rem(lax.axis_index("slab"), GROUP)
    column = 4 * member + lax.rem(lax.broadcasted_iota(jnp.int32, (48, LANES), 0), 4)
    for turn in range(4):
        source = data if turn == 0 else scratch.at[(turn - 1) % 2]
        target = out if turn == 3 else scratch.at[turn % 2]
        distance = jnp.left_shift(jnp.int32(1), bits[turn])
        for slab in range(GROUP):
            moved = column < taken[turn * GROUP + slab]
            target[slab] = jnp.where(moved, source[jnp.bitwise_xor(slab, distance)], source[slab])


def place_kernel(whole, columns, out):
    del whole
    rows = out.shape[2]
    for start in range(0, rows, 8):
        group = start // 4
        at = slice(start, start + 8)
        for c in range(3):
            for half in range(2):
                cells = slice(half * LANES, (half + 1) * LANES)
                low = c * 8 + half * 4
                part = slice(low, low + 4)
                for g in range(2):
                    at = slice(start + 4 * g, start + 4 * g + 4)
                    velocity = columns[group + g, part]
                    out[3 + c, 0, at, cells] = velocity
                    out[c, 0, at, cells] = columns[group + g, low + 24 : low + 28] + 0.1 * velocity


VMEM = pl.BlockSpec(memory_space=pltpu.VMEM)
SMEM = pl.BlockSpec(memory_space=pltpu.SMEM)
ALONE = pltpu.CompilerParams(vmem_limit_bytes=60 * 1024 * 1024)
PARAMS = pltpu.CompilerParams(vmem_limit_bytes=40 * 1024 * 1024)


def exchange(block):
    count = lax.axis_size("slab")
    groups = [list(range(g, g + GROUP)) for g in range(0, count, GROUP)]
    return lax.all_to_all(block, "slab", 0, 0, axis_index_groups=groups)


def on_device(displacement, velocity, damage, broken, counts, bits):
    planes, rows, cells = damage.shape
    f32 = jnp.float32
    shape = jax.ShapeDtypeStruct
    group_shape = (GROUP, 48, LANES)
    slabs = lax.axis_size("slab")
    upward = [(i, i + 1) for i in range(slabs - 1)]
    downward = [(i + 1, i) for i in range(slabs - 1)]
    across_up = [(2 * s + c, 2 * t + 1 - c) for s, t in upward for c in range(2)]
    across_down = [(2 * s + c, 2 * t + 1 - c) for s, t in downward for c in range(2)]
    both = ("slab", "col")
    anywhere = pl.BlockSpec(memory_space=pl.ANY)

    up, down, edge, edge_up, edge_down = pl.pallas_call(
        pack_kernel,
        out_shape=[
            shape((8, rows, cells), f32),
            shape((6, rows, cells), f32),
            shape((6, 2 * planes, cells), f32),
            shape((8, cells), f32),
            shape((8, cells), f32),
        ],
        in_specs=[pl.BlockSpec(memory_space=pltpu.HBM)] * 3,
        out_specs=[VMEM] * 5,
        scratch_shapes=[
            pltpu.VMEM((3, planes, 8, cells), f32),
            pltpu.VMEM((planes, 8, cells), f32),
            pltpu.VMEM((2, planes, 8, cells), jnp.int32),
            pltpu.VMEM((3, rows, cells), jnp.int32),
            pltpu.VMEM((rows, cells), f32),
            pltpu.SemaphoreType.DMA((18,)),
        ],
        compiler_params=ALONE,
        name="pack",
    )(displacement, damage, broken)
    up = lax.ppermute(up, "slab", upward)
    edge_up = lax.ppermute(edge_up, both, across_up)
    edge = lax.ppermute(edge, "col", [(0, 1), (1, 0)])
    down = lax.ppermute(down, "slab", downward)

    member = jnp.arange(GROUP, dtype=jnp.int32)
    base = lax.axis_index("slab") // GROUP * GROUP
    mine = lax.dynamic_slice_in_dim(counts, base, GROUP, 0).T
    partner = jnp.bitwise_xor(member[None, :], jnp.left_shift(jnp.int32(1), bits)[:, None])
    taken = jnp.minimum(mine, jnp.take_along_axis(mine, partner, axis=1)).reshape(-1)

    def forces(name, targets, low, high, out, **operands):
        slots = sum(low <= p < high for p in range(min(targets) - 1, max(targets) + 2))
        return pl.pallas_call(
            functools.partial(force_kernel, targets, low, high, tuple(operands)),
            out_shape=out,
            in_specs=[anywhere if key.startswith("order") else VMEM for key in operands],
            out_specs=VMEM,
            scratch_shapes=[
                pltpu.VMEM((4, 5, slots, 2, rows + 2 * TOP, LANES), f32),
                pltpu.VMEM((2, 5, slots, 2, rows + 2 * TOP, LANES), jnp.int32),
            ],
            compiler_params=PARAMS,
            name=name,
        )(*operands.values())

    own = dict(disp=displacement, damage=damage)
    begun = forces(
        "force_own", (0,), 0, planes, shape((3, 1, rows, cells), f32),
        vel=velocity, broken=broken, edge=edge, **own,
    )
    send = forces(
        "force_below", (0,), -2, 0, shape(group_shape, f32),
        vel=begun, up=up, edge_up=edge_up, order=down, **own,
    )
    edge_down, send = lax.optimization_barrier((edge_down, send))
    columns = exchange(send)
    edge_down = lax.ppermute(edge_down, both, across_down)

    whole = forces(
        "force_rest", tuple(range(1, planes)), -2, planes + 2, shape((6, planes, rows, cells), f32),
        vel=velocity, broken=broken, up=up, down=down, edge=edge, edge_up=edge_up,
        edge_down=edge_down, **own,
    )
    columns = pl.pallas_call(
        route_kernel,
        out_shape=shape(group_shape, f32),
        in_specs=[SMEM, SMEM, VMEM, anywhere],
        out_specs=VMEM,
        scratch_shapes=[pltpu.VMEM((2,) + group_shape, f32)],
        compiler_params=PARAMS,
        name="route",
    )(taken, bits, columns, edge_down)
    columns = exchange(columns)
    return pl.pallas_call(
        place_kernel,
        out_shape=shape((6, planes, rows, cells), f32),
        in_specs=[anywhere, pl.BlockSpec(group_shape, lambda i: (0, 0, 0))],
        out_specs=pl.BlockSpec((6, 1, rows, cells), lambda i: (0, 0, 0, 0)),
        grid=(1,),
        input_output_aliases={0: 0},
        compiler_params=PARAMS,
        name="place",
    )(whole, columns)


def solution(mesh):
    return jax.shard_map(
        on_device,
        mesh=mesh,
        in_specs=(
            P(None, "slab", "col", None),
            P(None, "slab", "col", None),
            P("slab", "col", None),
            P(None, "slab", "col", None),
            P(),
            P(),
        ),
        out_specs=P(None, "slab", "col", None),
        check_vma=False,
    )
```

```python
import functools
import math

import jax
import jax.numpy as jnp
from jax import lax
from jax.experimental import pallas as pl
from jax.experimental.pallas import tpu as pltpu
from jax.sharding import PartitionSpec as P

GROUP = 16
LANES = 128
TOP = 8


def bond_table():
    table = []
    for step_x in range(-2, 3):
        for step_y in range(-2, 3):
            for step_z in range(-2, 3):
                square = step_x * step_x + step_y * step_y + step_z * step_z
                if 0 < square <= 4 and (step_x, step_y, step_z) > (0, 0, 0):
                    length = math.sqrt(square)
                    table.append((step_x, step_y, step_z, (1.0 - length / 2.5) / length**3))
    return table


BONDS = bond_table()


def to_groups(ref, step, first, half, values):
    for c, value in enumerate(values):
        low = (first + c) * 8 + half * 4
        ref[2 * step, low : low + 4, :] = value[0:4]
        ref[2 * step + 1, low : low + 4, :] = value[4:8]


def alive_of(flags, index):
    return (flags & (1 << (index % 8))) == 0


def pack_kernel(
    disp, damage, broken, up, down, edge, edge_up, edge_down, disp_rim, damage_rim, words, flags,
    scale, sems
):
    position = lax.axis_index("col")
    planes, rows = damage.shape[0], damage.shape[1]
    last = planes - 1
    rim = pl.ds(pl.multiple_of((1 - position) * (rows - 8), 8), 8)
    moves = [
        (disp.at[:, :, rim], disp_rim),
        (damage.at[:, rim], damage_rim),
        (broken.at[:, :, rim], words),
        (disp.at[0, 1], down.at[4]),
        (damage.at[0], down.at[3]),
        (damage.at[1], down.at[5]),
    ]
    moves += [(disp.at[c, 0], down.at[c]) for c in range(3)]
    moves += [(disp.at[c, last], up.at[c]) for c in range(3)]
    moves += [(damage.at[last], up.at[3]), (disp.at[0, last - 1], up.at[6])]
    moves += [(broken.at[w, last], flags.at[w]) for w in range(2)]
    moves += [(broken.at[1, last - 1], flags.at[2]), (damage.at[last - 1], scale)]
    copies = [
        pltpu.make_async_copy(source, target, sems.at[i])
        for i, (source, target) in enumerate(moves)
    ]
    for copy in copies:
        copy.start()
    edge_up[...] = jnp.zeros(edge_up.shape, jnp.float32)
    edge_down[...] = jnp.zeros(edge_down.shape, jnp.float32)
    for copy in copies:
        copy.wait()
    up[4] = flags[0].astype(jnp.float32)
    up[5] = flags[1].astype(jnp.float32)
    up[7] = jnp.where(alive_of(flags[2], 15), scale[...], 0.0)

    def edges(first, inner):
        for plane in range(planes):
            at = slice(2 * plane, 2 * plane + 2)
            for c in range(3):
                edge[c, at] = disp_rim[c, plane, first : first + 2]
            edge[3, at] = damage_rim[plane, first : first + 2]
            for word in range(2):
                edge[4 + word, at] = words[word, plane, first : first + 2].astype(jnp.float32)
        one = slice(inner, inner + 1)
        for c in range(3):
            edge_up[c : c + 1] = disp_rim[c, last, one]
            edge_down[c : c + 1] = disp_rim[c, 0, one]
        edge_up[3:4] = damage_rim[last, one]
        edge_down[3:4] = damage_rim[0, one]
        for word in range(2):
            edge_up[4 + word : 5 + word] = words[word, last, one].astype(jnp.float32)

    @pl.when(position == 0)
    def _():
        edges(6, 7)

    @pl.when(position == 1)
    def _():
        edges(0, 0)


def fill(fields, flags, slot, values, words, rim, width, position, rows):
    lane = lax.broadcasted_iota(jnp.int32, (rows + 2 * TOP, LANES), 1)

    def base(ref, index, read, rim_read, dtype):
        ref[index, 2, slot, :, 0:TOP] = jnp.zeros((2, TOP, LANES), dtype)
        ref[index, 2, slot, :, TOP + rows :] = jnp.zeros((2, TOP, LANES), dtype)
        for half in range(2):
            cells = slice(half * LANES, (half + 1) * LANES)
            ref[index, 2, slot, half, TOP : TOP + rows] = read(cells)

        @pl.when(position == 0)
        def _():
            for half in range(2):
                cells = slice(half * LANES, (half + 1) * LANES)
                ref[index, 2, slot, half, TOP + rows : TOP + rows + width] = rim_read(cells)

        @pl.when(position == 1)
        def _():
            for half in range(2):
                cells = slice(half * LANES, (half + 1) * LANES)
                ref[index, 2, slot, half, TOP - width : TOP] = rim_read(cells)

    def shift(ref, index, amounts, zero):
        halves = [ref[index, 2, slot, half] for half in range(2)]
        for amount in amounts:
            rolled = [pltpu.roll(v, (-amount) % LANES, 1) for v in halves]
            crossed = lane >= LANES - amount if amount > 0 else lane < -amount
            edge = jnp.zeros_like(rolled[0]) if zero else rolled[0]
            if amount > 0:
                new = [jnp.where(crossed, rolled[1], rolled[0]), jnp.where(crossed, edge, rolled[1])]
            else:
                new = [jnp.where(crossed, edge, rolled[0]), jnp.where(crossed, rolled[0], rolled[1])]
            for half in range(2):
                ref[index, 2 + amount, slot, half] = new[half]

    for index, (read, rim_read) in enumerate(zip(values, rim[:4])):
        base(fields, index, read, rim_read, jnp.float32)
        shift(fields, index, (-2, -1, 1, 2) if index >= 2 else (-1, 1), index == 3)
    for index, (read, rim_read) in enumerate(zip(words, rim[4:])):
        base(flags, index, read, rim_read, jnp.int32)
        shift(flags, index, (-2, -1, 1) if index == 0 else (-1, 1), False)


def force_kernel(targets, low, high, names, *refs):
    ref_of = dict(zip(names, refs))
    out, fields, flags = refs[len(names) :]
    disp, vel, damage = ref_of["disp"], ref_of["vel"], ref_of["damage"]
    broken, up, down = ref_of.get("broken"), ref_of.get("up"), ref_of.get("down")
    edge, edge_up, edge_down = ref_of.get("edge"), ref_of.get("edge_up"), ref_of.get("edge_down")
    position = lax.axis_index("col")
    planes, rows = ref_of["damage"].shape[0], damage.shape[1]
    closing = high == 0
    needed = sorted({p + a for p in targets for a in (-1, 0, 1) if low <= p + a < high})
    slots = {p: slot for slot, p in enumerate(needed)}

    for p in needed:
        if p < 0:
            values = [lambda cells, c=c: up[c, :, cells] for c in range(4)]
            words = [lambda cells, w=w: up[4 + w, :, cells].astype(jnp.int32) for w in range(2)]
            rim = [lambda cells, c=c: edge_up[c : c + 1, cells] for c in range(4)]
            rim += [
                lambda cells, w=w: edge_up[4 + w : 5 + w, cells].astype(jnp.int32) for w in range(2)
            ]
            width = 1
        elif p >= planes:
            values = [lambda cells, c=c: down[c, :, cells] for c in range(4)]
            words = []
            rim = [lambda cells, c=c: edge_down[c : c + 1, cells] for c in range(4)]
            width = 1
        else:
            at = slice(2 * p, 2 * p + 2)
            values = [lambda cells, c=c, p=p: disp[c, p, :, cells] for c in range(3)]
            values += [lambda cells, p=p: damage[p, :, cells]]
            words = [lambda cells, w=w, p=p: broken[w, p, :, cells] for w in range(2)]
            rim = [lambda cells, c=c, at=at: edge[c, at, cells] for c in range(4)]
            rim += [
                lambda cells, w=w, at=at: edge[4 + w, at, cells].astype(jnp.int32) for w in range(2)
            ]
            width = 2
        fill(fields, flags, slots[p], values, words, rim, width, position, rows)

    def block(step, carry):
        start = pl.multiple_of(step * 8, 8)
        own_rows = pl.ds(start, 8)
        for p in targets:
            for half in range(2):
                cells = slice(half * LANES, (half + 1) * LANES)
                own = [disp[c, p, own_rows, cells] for c in range(3)]
                own_damage = damage[p, own_rows, cells]
                own_words = [broken[w, p, own_rows, cells] for w in range(2)] if not closing else []
                force = [None, None, None]

                def add(axis, value):
                    force[axis] = value if force[axis] is None else force[axis] + value

                for index, (step_x, step_y, step_z, weight) in enumerate(BONDS):
                    for sign in (1, -1):
                        if not low <= p + sign * step_x < high:
                            continue
                        if step_x == 2:
                            q = p + 2 * sign
                            if q == -2:
                                other, scale = up[6, own_rows, cells], up[7, own_rows, cells]
                            elif q == -1:
                                other, scale = up[0, own_rows, cells], up[3, own_rows, cells]
                                bits = up[5, own_rows, cells].astype(jnp.int32)
                                scale = jnp.where(alive_of(bits, index), scale, 0.0)
                            elif q == planes + 1:
                                other, scale = down[4, own_rows, cells], down[5, own_rows, cells]
                            elif q == planes:
                                other, scale = down[0, own_rows, cells], down[3, own_rows, cells]
                            else:
                                other, scale = disp[0, q, own_rows, cells], damage[q, own_rows, cells]
                                if sign == -1:
                                    bits = broken[1, q, own_rows, cells]
                                    scale = jnp.where(alive_of(bits, index), scale, 0.0)
                            if sign == 1:
                                scale = jnp.where(alive_of(own_words[1], index), scale, 0.0)
                            factor = (4.0 * weight) * scale * (other - own[0])
                            add(0, factor)
                            continue
                        slot = slots[p + sign * step_x]
                        at = pl.ds(start + TOP + sign * step_y, 8)
                        place = 2 + sign * step_z
                        steps = (step_x, step_y, step_z)
                        along = None
                        for axis in range(3):
                            if steps[axis] == 0:
                                continue
                            part = fields[axis, place, slot, half, at] - own[axis]
                            if abs(steps[axis]) == 2:
                                along = part
                            elif along is None:
                                along = part if steps[axis] == 1 else -part
                            else:
                                along = along + part if steps[axis] == 1 else along - part
                        scale = fields[3, place, slot, half, at]
                        if sign == 1:
                            bits = own_words[index // 8]
                        else:
                            bits = flags[index // 8, place, slot, half, at]
                        scale = jnp.where(alive_of(bits, index), scale, 0.0)
                        if max(abs(s) for s in steps) == 2:
                            factor = (4.0 * weight) * scale * along
                        else:
                            factor = weight * scale * along
                        for axis in range(3):
                            if steps[axis] > 0:
                                add(axis, factor)
                            elif steps[axis] < 0:
                                add(axis, -factor)
                new_velocity = [
                    vel[c, p, own_rows, cells] + 0.1 * (own_damage * force[c]) for c in range(3)
                ]
                if closing:
                    to_groups(out, step, 0, half, new_velocity)
                    to_groups(out, step, 3, half, own)
                elif targets == (0,):
                    for c in range(3):
                        out[c, 0, own_rows, cells] = new_velocity[c]
                else:
                    for c in range(3):
                        out[3 + c, p, own_rows, cells] = new_velocity[c]
                        out[c, p, own_rows, cells] = own[c] + 0.1 * new_velocity[c]
        return carry

    lax.fori_loop(0, rows // 8, block, 0)


def route_kernel(taken, bits, data, order, out, scratch):
    del order
    member = lax.rem(lax.axis_index("slab"), GROUP)
    column = 4 * member + lax.rem(lax.broadcasted_iota(jnp.int32, (48, LANES), 0), 4)
    for turn in range(4):
        source = data if turn == 0 else scratch.at[(turn - 1) % 2]
        target = out if turn == 3 else scratch.at[turn % 2]
        distance = jnp.left_shift(jnp.int32(1), bits[turn])
        for slab in range(GROUP):
            moved = column < taken[turn * GROUP + slab]
            target[slab] = jnp.where(moved, source[jnp.bitwise_xor(slab, distance)], source[slab])


def place_kernel(whole, columns, out):
    del whole
    rows = out.shape[2]
    for start in range(0, rows, 8):
        group = start // 4
        at = slice(start, start + 8)
        for c in range(3):
            for half in range(2):
                cells = slice(half * LANES, (half + 1) * LANES)
                low = c * 8 + half * 4
                part = slice(low, low + 4)
                for g in range(2):
                    at = slice(start + 4 * g, start + 4 * g + 4)
                    velocity = columns[group + g, part]
                    out[3 + c, 0, at, cells] = velocity
                    out[c, 0, at, cells] = columns[group + g, low + 24 : low + 28] + 0.1 * velocity


VMEM = pl.BlockSpec(memory_space=pltpu.VMEM)
SMEM = pl.BlockSpec(memory_space=pltpu.SMEM)
ALONE = pltpu.CompilerParams(vmem_limit_bytes=60 * 1024 * 1024)
PARAMS = pltpu.CompilerParams(vmem_limit_bytes=40 * 1024 * 1024)


def exchange(block):
    count = lax.axis_size("slab")
    groups = [list(range(g, g + GROUP)) for g in range(0, count, GROUP)]
    return lax.all_to_all(block, "slab", 0, 0, axis_index_groups=groups)


def on_device(displacement, velocity, damage, broken, counts, bits):
    planes, rows, cells = damage.shape
    f32 = jnp.float32
    shape = jax.ShapeDtypeStruct
    group_shape = (GROUP, 48, LANES)
    slabs = lax.axis_size("slab")
    upward = [(i, i + 1) for i in range(slabs - 1)]
    downward = [(i + 1, i) for i in range(slabs - 1)]
    across_up = [(2 * s + c, 2 * t + 1 - c) for s, t in upward for c in range(2)]
    across_down = [(2 * s + c, 2 * t + 1 - c) for s, t in downward for c in range(2)]
    both = ("slab", "col")
    anywhere = pl.BlockSpec(memory_space=pl.ANY)

    up, down, edge, edge_up, edge_down = pl.pallas_call(
        pack_kernel,
        out_shape=[
            shape((8, rows, cells), f32),
            shape((6, rows, cells), f32),
            shape((6, 2 * planes, cells), f32),
            shape((8, cells), f32),
            shape((8, cells), f32),
        ],
        in_specs=[pl.BlockSpec(memory_space=pltpu.HBM)] * 3,
        out_specs=[VMEM] * 5,
        scratch_shapes=[
            pltpu.VMEM((3, planes, 8, cells), f32),
            pltpu.VMEM((planes, 8, cells), f32),
            pltpu.VMEM((2, planes, 8, cells), jnp.int32),
            pltpu.VMEM((3, rows, cells), jnp.int32),
            pltpu.VMEM((rows, cells), f32),
            pltpu.SemaphoreType.DMA((18,)),
        ],
        compiler_params=ALONE,
        name="pack",
    )(displacement, damage, broken)
    up = lax.ppermute(up, "slab", upward)
    edge_up = lax.ppermute(edge_up, both, across_up)
    edge = lax.ppermute(edge, "col", [(0, 1), (1, 0)])
    down = lax.ppermute(down, "slab", downward)

    member = jnp.arange(GROUP, dtype=jnp.int32)
    base = lax.axis_index("slab") // GROUP * GROUP
    mine = lax.dynamic_slice_in_dim(counts, base, GROUP, 0).T
    partner = jnp.bitwise_xor(member[None, :], jnp.left_shift(jnp.int32(1), bits)[:, None])
    taken = jnp.minimum(mine, jnp.take_along_axis(mine, partner, axis=1)).reshape(-1)

    def forces(name, targets, low, high, out, **operands):
        slots = sum(low <= p < high for p in range(min(targets) - 1, max(targets) + 2))
        return pl.pallas_call(
            functools.partial(force_kernel, targets, low, high, tuple(operands)),
            out_shape=out,
            in_specs=[anywhere if key.startswith("order") else VMEM for key in operands],
            out_specs=VMEM,
            scratch_shapes=[
                pltpu.VMEM((4, 5, slots, 2, rows + 2 * TOP, LANES), f32),
                pltpu.VMEM((2, 5, slots, 2, rows + 2 * TOP, LANES), jnp.int32),
            ],
            compiler_params=PARAMS,
            name=name,
        )(*operands.values())

    own = dict(disp=displacement, damage=damage)
    begun = forces(
        "force_own", (0,), 0, planes, shape((3, 1, rows, cells), f32),
        vel=velocity, broken=broken, edge=edge, **own,
    )
    send = forces(
        "force_below", (0,), -2, 0, shape(group_shape, f32),
        vel=begun, up=up, edge_up=edge_up, order=down, **own,
    )
    edge_down, send = lax.optimization_barrier((edge_down, send))
    columns = exchange(send)
    edge_down = lax.ppermute(edge_down, both, across_down)

    whole = forces(
        "force_rest", tuple(range(1, planes)), -2, planes + 2, shape((6, planes, rows, cells), f32),
        vel=velocity, broken=broken, up=up, down=down, edge=edge, edge_up=edge_up,
        edge_down=edge_down, **own,
    )
    columns = pl.pallas_call(
        route_kernel,
        out_shape=shape(group_shape, f32),
        in_specs=[SMEM, SMEM, VMEM, anywhere],
        out_specs=VMEM,
        scratch_shapes=[pltpu.VMEM((2,) + group_shape, f32)],
        compiler_params=PARAMS,
        name="route",
    )(taken, bits, columns, edge_down)
    columns = exchange(columns)
    return pl.pallas_call(
        place_kernel,
        out_shape=shape((6, planes, rows, cells), f32),
        in_specs=[anywhere, pl.BlockSpec((GROUP // 4, 48, LANES), lambda i: (i, 0, 0))],
        out_specs=pl.BlockSpec((6, 1, rows // 4, cells), lambda i: (0, 0, i, 0)),
        grid=(4,),
        input_output_aliases={0: 0},
        compiler_params=PARAMS,
        name="place",
    )(whole, columns)


def solution(mesh):
    return jax.shard_map(
        on_device,
        mesh=mesh,
        in_specs=(
            P(None, "slab", "col", None),
            P(None, "slab", "col", None),
            P("slab", "col", None),
            P(None, "slab", "col", None),
            P(),
            P(),
        ),
        out_specs=P(None, "slab", "col", None),
        check_vma=False,
    )
```

```python
import functools
import math

import jax
import jax.numpy as jnp
from jax import lax
from jax.experimental import pallas as pl
from jax.experimental.pallas import tpu as pltpu
from jax.sharding import PartitionSpec as P

GROUP = 16
LANES = 128
TOP = 8


def bond_table():
    table = []
    for step_x in range(-2, 3):
        for step_y in range(-2, 3):
            for step_z in range(-2, 3):
                square = step_x * step_x + step_y * step_y + step_z * step_z
                if 0 < square <= 4 and (step_x, step_y, step_z) > (0, 0, 0):
                    length = math.sqrt(square)
                    table.append((step_x, step_y, step_z, (1.0 - length / 2.5) / length**3))
    return table


BONDS = bond_table()


def to_groups(ref, step, first, half, values):
    for c, value in enumerate(values):
        low = (first + c) * 8 + half * 4
        ref[2 * step, low : low + 4, :] = value[0:4]
        ref[2 * step + 1, low : low + 4, :] = value[4:8]


def alive_of(flags, index):
    return (flags & (1 << (index % 8))) == 0


def pack_kernel(
    disp, damage, broken, up, down, edge, edge_up, edge_down, disp_rim, damage_rim, words, flags,
    scale, sems
):
    position = lax.axis_index("col")
    planes, rows = damage.shape[0], damage.shape[1]
    last = planes - 1
    rim = pl.ds(pl.multiple_of((1 - position) * (rows - 8), 8), 8)
    moves = [
        (disp.at[:, :, rim], disp_rim),
        (damage.at[:, rim], damage_rim),
        (broken.at[:, :, rim], words),
        (disp.at[0, 1], down.at[4]),
        (damage.at[0], down.at[3]),
        (damage.at[1], down.at[5]),
    ]
    moves += [(disp.at[c, 0], down.at[c]) for c in range(3)]
    moves += [(disp.at[c, last], up.at[c]) for c in range(3)]
    moves += [(damage.at[last], up.at[3]), (disp.at[0, last - 1], up.at[6])]
    moves += [(broken.at[w, last], flags.at[w]) for w in range(2)]
    moves += [(broken.at[1, last - 1], flags.at[2]), (damage.at[last - 1], scale)]
    copies = [
        pltpu.make_async_copy(source, target, sems.at[i])
        for i, (source, target) in enumerate(moves)
    ]
    for copy in copies:
        copy.start()
    edge_up[...] = jnp.zeros(edge_up.shape, jnp.float32)
    edge_down[...] = jnp.zeros(edge_down.shape, jnp.float32)
    for copy in copies:
        copy.wait()
    up[4] = flags[0].astype(jnp.float32)
    up[5] = flags[1].astype(jnp.float32)
    up[7] = jnp.where(alive_of(flags[2], 15), scale[...], 0.0)

    def edges(first, inner):
        for plane in range(planes):
            at = slice(2 * plane, 2 * plane + 2)
            for c in range(3):
                edge[c, at] = disp_rim[c, plane, first : first + 2]
            edge[3, at] = damage_rim[plane, first : first + 2]
            for word in range(2):
                edge[4 + word, at] = words[word, plane, first : first + 2].astype(jnp.float32)
        one = slice(inner, inner + 1)
        for c in range(3):
            edge_up[c : c + 1] = disp_rim[c, last, one]
            edge_down[c : c + 1] = disp_rim[c, 0, one]
        edge_up[3:4] = damage_rim[last, one]
        edge_down[3:4] = damage_rim[0, one]
        for word in range(2):
            edge_up[4 + word : 5 + word] = words[word, last, one].astype(jnp.float32)

    @pl.when(position == 0)
    def _():
        edges(6, 7)

    @pl.when(position == 1)
    def _():
        edges(0, 0)


def fill(fields, flags, slot, values, words, rim, width, position, rows):
    lane = lax.broadcasted_iota(jnp.int32, (rows + 2 * TOP, LANES), 1)

    def base(ref, index, read, rim_read, dtype):
        ref[index, 2, slot, :, 0:TOP] = jnp.zeros((2, TOP, LANES), dtype)
        ref[index, 2, slot, :, TOP + rows :] = jnp.zeros((2, TOP, LANES), dtype)
        for half in range(2):
            cells = slice(half * LANES, (half + 1) * LANES)
            ref[index, 2, slot, half, TOP : TOP + rows] = read(cells)

        @pl.when(position == 0)
        def _():
            for half in range(2):
                cells = slice(half * LANES, (half + 1) * LANES)
                ref[index, 2, slot, half, TOP + rows : TOP + rows + width] = rim_read(cells)

        @pl.when(position == 1)
        def _():
            for half in range(2):
                cells = slice(half * LANES, (half + 1) * LANES)
                ref[index, 2, slot, half, TOP - width : TOP] = rim_read(cells)

    def shift(ref, index, amounts, zero):
        halves = [ref[index, 2, slot, half] for half in range(2)]
        for amount in amounts:
            rolled = [pltpu.roll(v, (-amount) % LANES, 1) for v in halves]
            crossed = lane >= LANES - amount if amount > 0 else lane < -amount
            edge = jnp.zeros_like(rolled[0]) if zero else rolled[0]
            if amount > 0:
                new = [jnp.where(crossed, rolled[1], rolled[0]), jnp.where(crossed, edge, rolled[1])]
            else:
                new = [jnp.where(crossed, edge, rolled[0]), jnp.where(crossed, rolled[0], rolled[1])]
            for half in range(2):
                ref[index, 2 + amount, slot, half] = new[half]

    for index, (read, rim_read) in enumerate(zip(values, rim[:4])):
        base(fields, index, read, rim_read, jnp.float32)
        shift(fields, index, (-2, -1, 1, 2) if index >= 2 else (-1, 1), index == 3)
    for index, (read, rim_read) in enumerate(zip(words, rim[4:])):
        base(flags, index, read, rim_read, jnp.int32)
        shift(flags, index, (-2, -1, 1) if index == 0 else (-1, 1), False)


def force_kernel(targets, low, high, names, *refs):
    ref_of = dict(zip(names, refs))
    out, fields, flags = refs[len(names) :]
    disp, vel, damage = ref_of["disp"], ref_of["vel"], ref_of["damage"]
    broken, up, down = ref_of.get("broken"), ref_of.get("up"), ref_of.get("down")
    edge, edge_up, edge_down = ref_of.get("edge"), ref_of.get("edge_up"), ref_of.get("edge_down")
    position = lax.axis_index("col")
    planes, rows = ref_of["damage"].shape[0], damage.shape[1]
    closing = high == 0
    needed = sorted({p + a for p in targets for a in (-1, 0, 1) if low <= p + a < high})
    slots = {p: slot for slot, p in enumerate(needed)}

    for p in needed:
        if p < 0:
            values = [lambda cells, c=c: up[c, :, cells] for c in range(4)]
            words = [lambda cells, w=w: up[4 + w, :, cells].astype(jnp.int32) for w in range(2)]
            rim = [lambda cells, c=c: edge_up[c : c + 1, cells] for c in range(4)]
            rim += [
                lambda cells, w=w: edge_up[4 + w : 5 + w, cells].astype(jnp.int32) for w in range(2)
            ]
            width = 1
        elif p >= planes:
            values = [lambda cells, c=c: down[c, :, cells] for c in range(4)]
            words = []
            rim = [lambda cells, c=c: edge_down[c : c + 1, cells] for c in range(4)]
            width = 1
        else:
            at = slice(2 * p, 2 * p + 2)
            values = [lambda cells, c=c, p=p: disp[c, p, :, cells] for c in range(3)]
            values += [lambda cells, p=p: damage[p, :, cells]]
            words = [lambda cells, w=w, p=p: broken[w, p, :, cells] for w in range(2)]
            rim = [lambda cells, c=c, at=at: edge[c, at, cells] for c in range(4)]
            rim += [
                lambda cells, w=w, at=at: edge[4 + w, at, cells].astype(jnp.int32) for w in range(2)
            ]
            width = 2
        fill(fields, flags, slots[p], values, words, rim, width, position, rows)

    def block(step, carry):
        start = pl.multiple_of(step * 8, 8)
        own_rows = pl.ds(start, 8)
        for p in targets:
            for half in range(2):
                cells = slice(half * LANES, (half + 1) * LANES)
                own = [disp[c, p, own_rows, cells] for c in range(3)]
                own_damage = damage[p, own_rows, cells]
                own_words = [broken[w, p, own_rows, cells] for w in range(2)] if not closing else []
                force = [None, None, None]

                def add(axis, value):
                    force[axis] = value if force[axis] is None else force[axis] + value

                for index, (step_x, step_y, step_z, weight) in enumerate(BONDS):
                    for sign in (1, -1):
                        if not low <= p + sign * step_x < high:
                            continue
                        if step_x == 2:
                            q = p + 2 * sign
                            if q == -2:
                                other, scale = up[6, own_rows, cells], up[7, own_rows, cells]
                            elif q == -1:
                                other, scale = up[0, own_rows, cells], up[3, own_rows, cells]
                                bits = up[5, own_rows, cells].astype(jnp.int32)
                                scale = jnp.where(alive_of(bits, index), scale, 0.0)
                            elif q == planes + 1:
                                other, scale = down[4, own_rows, cells], down[5, own_rows, cells]
                            elif q == planes:
                                other, scale = down[0, own_rows, cells], down[3, own_rows, cells]
                            else:
                                other, scale = disp[0, q, own_rows, cells], damage[q, own_rows, cells]
                                if sign == -1:
                                    bits = broken[1, q, own_rows, cells]
                                    scale = jnp.where(alive_of(bits, index), scale, 0.0)
                            if sign == 1:
                                scale = jnp.where(alive_of(own_words[1], index), scale, 0.0)
                            factor = (4.0 * weight) * scale * (other - own[0])
                            add(0, factor)
                            continue
                        slot = slots[p + sign * step_x]
                        at = pl.ds(start + TOP + sign * step_y, 8)
                        place = 2 + sign * step_z
                        steps = (step_x, step_y, step_z)
                        along = None
                        for axis in range(3):
                            if steps[axis] == 0:
                                continue
                            part = fields[axis, place, slot, half, at] - own[axis]
                            if abs(steps[axis]) == 2:
                                along = part
                            elif along is None:
                                along = part if steps[axis] == 1 else -part
                            else:
                                along = along + part if steps[axis] == 1 else along - part
                        scale = fields[3, place, slot, half, at]
                        if sign == 1:
                            bits = own_words[index // 8]
                        else:
                            bits = flags[index // 8, place, slot, half, at]
                        scale = jnp.where(alive_of(bits, index), scale, 0.0)
                        if max(abs(s) for s in steps) == 2:
                            factor = (4.0 * weight) * scale * along
                        else:
                            factor = weight * scale * along
                        for axis in range(3):
                            if steps[axis] > 0:
                                add(axis, factor)
                            elif steps[axis] < 0:
                                add(axis, -factor)
                new_velocity = [
                    vel[c, p, own_rows, cells] + 0.1 * (own_damage * force[c]) for c in range(3)
                ]
                if closing:
                    to_groups(out, step, 0, half, new_velocity)
                    to_groups(out, step, 3, half, own)
                elif targets == (0,):
                    for c in range(3):
                        out[c, 0, own_rows, cells] = new_velocity[c]
                else:
                    for c in range(3):
                        out[3 + c, p, own_rows, cells] = new_velocity[c]
                        out[c, p, own_rows, cells] = own[c] + 0.1 * new_velocity[c]
        return carry

    lax.fori_loop(0, rows // 8, block, 0)


def route_kernel(taken, bits, data, order, out, scratch, sems):
    del order
    member = lax.rem(lax.axis_index("slab"), GROUP)
    column = 4 * member + lax.rem(lax.broadcasted_iota(jnp.int32, (48, LANES), 0), 4)
    copies = []
    for turn in range(4):
        source = data if turn == 0 else scratch.at[(turn - 1) % 2]
        target = scratch.at[turn % 2]
        distance = jnp.left_shift(jnp.int32(1), bits[turn])
        for slab in range(GROUP):
            moved = column < taken[turn * GROUP + slab]
            target[slab] = jnp.where(moved, source[jnp.bitwise_xor(slab, distance)], source[slab])
            if turn == 3:
                copies.append(pltpu.make_async_copy(target.at[slab], out.at[slab], sems.at[slab]))
                copies[-1].start()
    for copy in copies:
        copy.wait()


def place_kernel(whole, columns, out):
    del whole
    rows = out.shape[2]
    for start in range(0, rows, 8):
        group = start // 4
        at = slice(start, start + 8)
        for c in range(3):
            for half in range(2):
                cells = slice(half * LANES, (half + 1) * LANES)
                low = c * 8 + half * 4
                part = slice(low, low + 4)
                for g in range(2):
                    at = slice(start + 4 * g, start + 4 * g + 4)
                    velocity = columns[group + g, part]
                    out[3 + c, 0, at, cells] = velocity
                    out[c, 0, at, cells] = columns[group + g, low + 24 : low + 28] + 0.1 * velocity


VMEM = pl.BlockSpec(memory_space=pltpu.VMEM)
SMEM = pl.BlockSpec(memory_space=pltpu.SMEM)
ALONE = pltpu.CompilerParams(vmem_limit_bytes=60 * 1024 * 1024)
PARAMS = pltpu.CompilerParams(vmem_limit_bytes=40 * 1024 * 1024)


def exchange(block):
    count = lax.axis_size("slab")
    groups = [list(range(g, g + GROUP)) for g in range(0, count, GROUP)]
    return lax.all_to_all(block, "slab", 0, 0, axis_index_groups=groups)


def on_device(displacement, velocity, damage, broken, counts, bits):
    planes, rows, cells = damage.shape
    f32 = jnp.float32
    shape = jax.ShapeDtypeStruct
    group_shape = (GROUP, 48, LANES)
    slabs = lax.axis_size("slab")
    upward = [(i, i + 1) for i in range(slabs - 1)]
    downward = [(i + 1, i) for i in range(slabs - 1)]
    across_up = [(2 * s + c, 2 * t + 1 - c) for s, t in upward for c in range(2)]
    across_down = [(2 * s + c, 2 * t + 1 - c) for s, t in downward for c in range(2)]
    both = ("slab", "col")
    anywhere = pl.BlockSpec(memory_space=pl.ANY)

    up, down, edge, edge_up, edge_down = pl.pallas_call(
        pack_kernel,
        out_shape=[
            shape((8, rows, cells), f32),
            shape((6, rows, cells), f32),
            shape((6, 2 * planes, cells), f32),
            shape((8, cells), f32),
            shape((8, cells), f32),
        ],
        in_specs=[pl.BlockSpec(memory_space=pltpu.HBM)] * 3,
        out_specs=[VMEM] * 5,
        scratch_shapes=[
            pltpu.VMEM((3, planes, 8, cells), f32),
            pltpu.VMEM((planes, 8, cells), f32),
            pltpu.VMEM((2, planes, 8, cells), jnp.int32),
            pltpu.VMEM((3, rows, cells), jnp.int32),
            pltpu.VMEM((rows, cells), f32),
            pltpu.SemaphoreType.DMA((18,)),
        ],
        compiler_params=ALONE,
        name="pack",
    )(displacement, damage, broken)
    up = lax.ppermute(up, "slab", upward)
    edge_up = lax.ppermute(edge_up, both, across_up)
    edge = lax.ppermute(edge, "col", [(0, 1), (1, 0)])
    down = lax.ppermute(down, "slab", downward)

    member = jnp.arange(GROUP, dtype=jnp.int32)
    base = lax.axis_index("slab") // GROUP * GROUP
    mine = lax.dynamic_slice_in_dim(counts, base, GROUP, 0).T
    partner = jnp.bitwise_xor(member[None, :], jnp.left_shift(jnp.int32(1), bits)[:, None])
    taken = jnp.minimum(mine, jnp.take_along_axis(mine, partner, axis=1)).reshape(-1)

    def forces(name, targets, low, high, out, **operands):
        slots = sum(low <= p < high for p in range(min(targets) - 1, max(targets) + 2))
        return pl.pallas_call(
            functools.partial(force_kernel, targets, low, high, tuple(operands)),
            out_shape=out,
            in_specs=[anywhere if key.startswith("order") else VMEM for key in operands],
            out_specs=VMEM,
            scratch_shapes=[
                pltpu.VMEM((4, 5, slots, 2, rows + 2 * TOP, LANES), f32),
                pltpu.VMEM((2, 5, slots, 2, rows + 2 * TOP, LANES), jnp.int32),
            ],
            compiler_params=PARAMS,
            name=name,
        )(*operands.values())

    own = dict(disp=displacement, damage=damage)
    begun = forces(
        "force_own", (0,), 0, planes, shape((3, 1, rows, cells), f32),
        vel=velocity, broken=broken, edge=edge, **own,
    )
    send = forces(
        "force_below", (0,), -2, 0, shape(group_shape, f32),
        vel=begun, up=up, edge_up=edge_up, order=down, **own,
    )
    edge_down, send = lax.optimization_barrier((edge_down, send))
    columns = exchange(send)
    edge_down = lax.ppermute(edge_down, both, across_down)

    whole = forces(
        "force_rest", tuple(range(1, planes)), -2, planes + 2, shape((6, planes, rows, cells), f32),
        vel=velocity, broken=broken, up=up, down=down, edge=edge, edge_up=edge_up,
        edge_down=edge_down, **own,
    )
    columns = pl.pallas_call(
        route_kernel,
        out_shape=shape(group_shape, f32),
        in_specs=[SMEM, SMEM, VMEM, anywhere],
        out_specs=anywhere,
        scratch_shapes=[pltpu.VMEM((2,) + group_shape, f32), pltpu.SemaphoreType.DMA((GROUP,))],
        compiler_params=ALONE,
        name="route",
    )(taken, bits, columns, edge_down)
    columns = exchange(columns)
    return pl.pallas_call(
        place_kernel,
        out_shape=shape((6, planes, rows, cells), f32),
        in_specs=[anywhere, pl.BlockSpec(group_shape, lambda i: (0, 0, 0))],
        out_specs=pl.BlockSpec((6, 1, rows, cells), lambda i: (0, 0, 0, 0)),
        grid=(1,),
        input_output_aliases={0: 0},
        compiler_params=PARAMS,
        name="place",
    )(whole, columns)


def solution(mesh):
    return jax.shard_map(
        on_device,
        mesh=mesh,
        in_specs=(
            P(None, "slab", "col", None),
            P(None, "slab", "col", None),
            P("slab", "col", None),
            P(None, "slab", "col", None),
            P(),
            P(),
        ),
        out_specs=P(None, "slab", "col", None),
        check_vma=False,
    )
```
